256 devices in a mesh: lat: 64 (over y, z_hi, x, core), lon: 4 (over z_lo).
Axes of the slice: x: 4, y: 4, z: 8 (z_hi: 2, z_lo: 4; z = z_hi * 4 + z_lo), core: 2. Of those that a mesh axis runs over, the one named last changes fastest.
Arguments:
- fields: bfloat16 [512, 128, 2, 512], P('lat', 'lon'), may hold values from -16 to 16
- qkv_weight: bfloat16 [512, 1536], replicated, may hold values from -5 to 5
- out_weight: bfloat16 [512, 512], replicated, may hold values from -0.25 to 0.25
- merge_weight: bfloat16 [2048, 1024], replicated, may hold values from -0.125 to 0.125
- cotangent: bfloat16 [256, 64, 2, 1024], P('lat', 'lon'), may hold values from -16 to 16
Outputs:
- merged: bfloat16 [256, 64, 2, 1024], P('lat', 'lon')
- field_grad: bfloat16 [512, 128, 2, 512], P('lat', 'lon')
- qkv_grad: float32 [512, 1536], P('lat', 'lon')
- out_grad: float32 [512, 512], P('lat', 'lon')
- merge_grad: float32 [2048, 1024], P('lat', 'lon')
The draws below stay inside these ranges and needn't reach their ends.
All inputs are finite; a program needn't handle non-finite values.
Results may differ from the reference program's by a relative error of at most 0.035.
The reference program's roundings to bfloat16 on the way count: a program that leaves them out, or rounds other values in their place, can miss the bound.
Values may be sent and summed in bfloat16 or wider, within the bound.
No kernel may reach another device: no remote copies, remote signals or barrier semaphores. Data moves between devices by JAX's collectives and lax.ppermute only.
A program may use at most 128 MiB of HBM per device.

```python
import math
import jax
import jax.numpy as jnp
from jax import lax

D = 512
HEADS = 8
LEVELS = 2
LAT_ALL = 512
LON_ALL = 128


def draw_qkv_weight(key, part):
    key = jax.random.fold_in(key, 11)
    base_key = jax.random.fold_in(key, 0)
    spread = 1.0 / math.sqrt(D)
    base = jax.random.truncated_normal(base_key, -4.0, 4.0, (D, 3 * D), jnp.float32)
    return (base * spread).astype(jnp.bfloat16)


def strengthened(values, key, source, target, blocks, factor):
    def block_of(position):
        return (jnp.arange(values.shape[position]) // (values.shape[position] // blocks)).reshape((-1,) + (1,) * (values.ndim - 1 - position))

    near = jax.random.permutation(key, blocks)[block_of(target)]
    other_side = (block_of(target) + blocks // 2) % blocks
    return jnp.where((block_of(source) == near) | (block_of(source) == other_side), factor * values, values)


def block_levels(stream_key, shape, shards, low, top_value):
    factor_of = 1.0
    for dim, parts in shards:
        heights = jax.random.uniform(jax.random.fold_in(jax.random.fold_in(stream_key, 6), dim), (parts,), jnp.float32, low / len(shards), top_value / len(shards))
        factor_of = factor_of * jnp.repeat(jnp.exp(heights), shape[dim] // parts).reshape((-1,) + (1,) * (len(shape) - 1 - dim))
    return factor_of


def centred(rng, extent, scale, bound, pieces=(), kind=jnp.bfloat16):
    entries = jax.random.normal(rng, extent, jnp.float32) * scale
    if len(pieces) > 0:
        entries = block_levels(rng, extent, pieces, -0.22, 0.18) * entries
    return jnp.clip(entries, min=-bound, max=bound).astype(kind)


def bell_draw_with(key, extent, scale, bound, pieces, heavy, kind=jnp.bfloat16):
    entries = scale * jax.random.normal(key, extent, jnp.float32)
    if pieces:
        entries = entries * block_levels(key, extent, pieces, -0.22, 0.18)
    return jnp.clip(strengthened(entries, jax.random.fold_in(key, 3), *heavy), -bound, bound).astype(kind)


def setup_inputs(seed: int = 0) -> dict:
    key_list = jax.random.split(jax.random.key(seed), 6)
    return {
        "fields": bell_draw_with(key_list[0], (LAT_ALL, LON_ALL, LEVELS, D), 1.0, 16.0, ((0, 64), (1, 4)), (0, 3, 64, 4.0)),
        "qkv_weight": draw_qkv_weight(jax.random.fold_in(key_list[5], 71), 0),
        "out_weight": centred(key_list[2], (D, D), D ** -0.5, 0.25),
        "merge_weight": centred(key_list[3], (4 * D, 2 * D), (4 * D) ** -0.5, 0.125),
        "cotangent": bell_draw_with(key_list[4], (LAT_ALL // 2, LON_ALL // 2, LEVELS, 2 * D), 1.0, 16.0, ((0, 64), (1, 4)), (0, 3, 64, 4.0)),
    }


def norm_rows(values):
    center = values - lax.optimization_barrier(jnp.mean(values, axis=-1, keepdims=True))
    spread = lax.optimization_barrier(jnp.mean(center * center, axis=-1, keepdims=True))
    return (center * lax.rsqrt(spread + 1e-05)).astype(jnp.bfloat16)

def to_windows(tensor):
    height, breadth, levels, width = tensor.shape
    shaped = tensor.reshape(height // 8, 8, breadth // 8, 8, levels // 2, 2, width)
    return shaped.transpose(0, 2, 4, 1, 3, 5, 6).reshape(-1, 128, width)

def from_windows(tensor, height, breadth, levels):
    width = tensor.shape[-1]
    shaped = tensor.reshape(height // 8, breadth // 8, levels // 2, 8, 8, 2, width)
    return shaped.transpose(0, 3, 1, 4, 2, 5, 6).reshape(height, breadth, levels, width)

def merge_cells(tensor):
    height, breadth, levels, width = tensor.shape
    shaped = tensor.reshape(height // 2, 2, breadth // 2, 2, levels, width)
    return shaped.transpose(0, 2, 4, 3, 1, 5).reshape(height // 2, breadth // 2, levels, 4 * width)

def split_cells(tensor):
    half_h, half_b, levels, wide = tensor.shape
    width = wide // 4
    shaped = tensor.reshape(half_h, half_b, levels, 2, 2, width)
    return shaped.transpose(0, 4, 1, 3, 2, 5).reshape(2 * half_h, 2 * half_b, levels, width)

def token_sum(left, right):
    left_flat = left.reshape(-1, left.shape[-1])
    right_flat = right.reshape(-1, right.shape[-1])
    return lax.dot_general(left_flat, right_flat, (((0,), (0,)), ((), ())), preferred_element_type=jnp.float32)

def back_product(tensor, weight):
    return lax.dot_general(tensor, weight, (((tensor.ndim - 1,), (1,)), ((), ())), preferred_element_type=jnp.float32)

def attend(qkv, region):
    windows, tokens, triple = qkv.shape
    width = triple // 3
    heads = HEADS
    split = qkv.reshape(windows, tokens, 3, heads, width // heads).astype(jnp.bfloat16)
    query = split[:, :, 0].astype(jnp.float32)
    keys = split[:, :, 1].astype(jnp.float32)
    values = split[:, :, 2].astype(jnp.float32)
    scores = jnp.einsum('wphd,wqhd->whpq', query, keys) / jnp.sqrt(jnp.float32(width // heads))
    allowed = region[:, :, None] == region[:, None, :]
    scores = jnp.where(allowed[:, None], scores, jnp.float32(-1000000000.0))
    probs = jax.nn.softmax(scores, axis=-1).astype(jnp.bfloat16)
    output = jnp.einsum('whpq,wqhd->wphd', probs.astype(jnp.float32), values)
    return output.reshape(windows, tokens, width).astype(jnp.bfloat16)

def band_region(band):
    row_ids = lax.broadcasted_iota(jnp.int32, (8, LON_ALL, LEVELS, 1), 0)
    flags = ((row_ids >= 4) & (band == LAT_ALL // 8 - 1)).astype(jnp.int32)
    return to_windows(flags)[..., 0]

def reference(fields, qkv_weight, out_weight, merge_weight, cotangent):
    fields_f = fields.astype(jnp.float32)
    rolled = jnp.roll(fields, (-4, -4), (0, 1)).reshape(LAT_ALL // 8, 8, LON_ALL, LEVELS, D)
    bands = jnp.arange(LAT_ALL // 8, dtype=jnp.int32)

    def forward_band(packed):
        band, tokens = packed
        normed = norm_rows(to_windows(tokens.astype(jnp.float32)))
        qkv = jnp.dot(normed, qkv_weight, preferred_element_type=jnp.float32)
        attended = attend(qkv, band_region(band))
        proj = jnp.dot(attended, out_weight, preferred_element_type=jnp.float32)
        return from_windows(proj, 8, LON_ALL, LEVELS)
    proj = lax.map(forward_band, (bands, rolled)).reshape(LAT_ALL, LON_ALL, LEVELS, D)
    proj = jnp.roll(proj, (4, 4), (0, 1))
    block = (fields_f + proj).astype(jnp.bfloat16)
    normed4, norm4_back = jax.vjp(norm_rows, merge_cells(block.astype(jnp.float32)))
    merged = jnp.dot(normed4, merge_weight, preferred_element_type=jnp.float32).astype(jnp.bfloat16)
    merge_grad = token_sum(normed4, cotangent)
    d_normed4 = back_product(cotangent, merge_weight).astype(jnp.bfloat16)
    d_block = split_cells(norm4_back(d_normed4)[0]).astype(jnp.bfloat16)
    d_rolled_in = jnp.roll(d_block, (-4, -4), (0, 1)).reshape(LAT_ALL // 8, 8, LON_ALL, LEVELS, D)

    def backward_band(packed):
        band, tokens, grads = packed
        window_in = to_windows(tokens.astype(jnp.float32))
        normed, norm_back = jax.vjp(norm_rows, window_in)
        qkv = jnp.dot(normed, qkv_weight, preferred_element_type=jnp.float32)
        region = band_region(band)
        attended, attend_back = jax.vjp(lambda inner: attend(inner, region), qkv)
        d_proj = to_windows(grads)
        out_term = token_sum(attended, d_proj)
        d_attended = back_product(d_proj, out_weight).astype(jnp.bfloat16)
        d_qkv = attend_back(d_attended)[0].astype(jnp.bfloat16)
        qkv_term = token_sum(normed, d_qkv)
        d_normed = back_product(d_qkv, qkv_weight).astype(jnp.bfloat16)
        d_window = norm_back(d_normed)[0]
        return (from_windows(d_window, 8, LON_ALL, LEVELS), qkv_term, out_term)
    d_rolled, qkv_terms, out_terms = lax.map(backward_band, (bands, rolled, d_rolled_in))
    d_rolled = jnp.roll(d_rolled.reshape(LAT_ALL, LON_ALL, LEVELS, D), (4, 4), (0, 1))
    field_grad = (d_block.astype(jnp.float32) + d_rolled).astype(jnp.bfloat16)
    qkv_grad = lax.optimization_barrier(jnp.sum(qkv_terms, axis=0))
    out_grad = lax.optimization_barrier(jnp.sum(out_terms, axis=0))
    return (merged, field_grad, qkv_grad, out_grad, merge_grad)
```

```python
import numpy as np
import jax
import jax.numpy as jnp
from jax import lax
from jax.sharding import Mesh, PartitionSpec as P

HEADS = 8
LAT = ("y", "zh", "x", "c")
ALL = ("y", "zh", "x", "c", "zl")
Z = ("zh", "zl")


def norm_rows(values):
    center = values - jnp.mean(values, axis=-1, keepdims=True)
    spread = jnp.mean(center * center, axis=-1, keepdims=True)
    return (center * lax.rsqrt(spread + 1e-05)).astype(jnp.bfloat16)


def to_windows(tensor):
    height, breadth, levels, width = tensor.shape
    shaped = tensor.reshape(height // 8, 8, breadth // 8, 8, levels // 2, 2, width)
    return shaped.transpose(0, 2, 4, 1, 3, 5, 6).reshape(-1, 128, width)


def from_windows(tensor, height, breadth, levels):
    width = tensor.shape[-1]
    shaped = tensor.reshape(height // 8, breadth // 8, levels // 2, 8, 8, 2, width)
    return shaped.transpose(0, 3, 1, 4, 2, 5, 6).reshape(height, breadth, levels, width)


def merge_cells(tensor):
    height, breadth, levels, width = tensor.shape
    shaped = tensor.reshape(height // 2, 2, breadth // 2, 2, levels, width)
    return shaped.transpose(0, 2, 4, 3, 1, 5).reshape(height // 2, breadth // 2, levels, 4 * width)


def split_cells(tensor):
    half_h, half_b, levels, wide = tensor.shape
    width = wide // 4
    shaped = tensor.reshape(half_h, half_b, levels, 2, 2, width)
    return shaped.transpose(0, 4, 1, 3, 2, 5).reshape(2 * half_h, 2 * half_b, levels, width)


def token_sum(left, right):
    left_flat = left.reshape(-1, left.shape[-1])
    right_flat = right.reshape(-1, right.shape[-1])
    return lax.dot_general(
        left_flat, right_flat, (((0,), (0,)), ((), ())), preferred_element_type=jnp.float32
    )


def back_product(tensor, weight):
    return lax.dot_general(
        tensor, weight, (((tensor.ndim - 1,), (1,)), ((), ())), preferred_element_type=jnp.float32
    )


def attend(qkv, region):
    windows, tokens, triple = qkv.shape
    width = triple // 3
    heads = HEADS
    split = qkv.reshape(windows, tokens, 3, heads, width // heads).astype(jnp.bfloat16)
    query = split[:, :, 0]
    keys = split[:, :, 1]
    values = split[:, :, 2]
    scores = jnp.einsum("wphd,wqhd->whpq", query, keys, preferred_element_type=jnp.float32)
    scores = scores / jnp.sqrt(jnp.float32(width // heads))
    allowed = region[:, :, None] == region[:, None, :]
    scores = jnp.where(allowed[:, None], scores, jnp.float32(-1000000000.0))
    probs = jax.nn.softmax(scores, axis=-1).astype(jnp.bfloat16)
    output = jnp.einsum("whpq,wqhd->wphd", probs, values, preferred_element_type=jnp.float32)
    return output.reshape(windows, tokens, width).astype(jnp.bfloat16)


def ring(axes, by):
    count = lax.axis_size(axes)
    return [(i, (i + by) % count) for i in range(count)]


def diagonal(by):
    lats, lons = lax.axis_size(LAT), lax.axis_size("zl")
    return [
        (i * lons + j, (i + by) % lats * lons + (j + by) % lons)
        for i in range(lats)
        for j in range(lons)
    ]


def halo_in(t, h):
    below = lax.ppermute(t[:h], LAT, ring(LAT, -1))
    right = lax.ppermute(t[h:, :h], "zl", ring("zl", -1))
    corner = lax.ppermute(t[:h, :h], ALL, diagonal(-1))
    top = jnp.concatenate([t[h:, h:], right], axis=1)
    bottom = jnp.concatenate([below[:, h:], corner], axis=1)
    return jnp.concatenate([top, bottom], axis=0)


def halo_out(t, h):
    w = t.shape[1] - h
    above = lax.ppermute(t[h:, :w], LAT, ring(LAT, 1))
    left = lax.ppermute(t[:h, w:], "zl", ring("zl", 1))
    corner = lax.ppermute(t[h:, w:], ALL, diagonal(1))
    top = jnp.concatenate([corner, above], axis=1)
    bottom = jnp.concatenate([left, t[:h, :w]], axis=1)
    return jnp.concatenate([top, bottom], axis=0)


def scatter_sum(blocks, axes):
    count = lax.axis_size(axes)
    me = lax.axis_index(axes)
    blocks = blocks.astype(jnp.bfloat16)
    total = lax.dynamic_index_in_dim(blocks, me, 0, False).astype(jnp.float32)
    for by in range(1, count):
        piece = lax.dynamic_index_in_dim(blocks, lax.rem(me + by, count), 0, False)
        total = total + lax.ppermute(piece, axes, ring(axes, by)).astype(jnp.float32)
    return total


def local(fields, qkv_weight, out_weight, merge_weight, cotangent):
    height, breadth, levels, width = fields.shape
    at_pole = lax.axis_index(LAT) == lax.axis_size(LAT) - 1
    row_ids = lax.broadcasted_iota(jnp.int32, (height, breadth, levels, 1), 0)
    region = to_windows(((row_ids >= height - 4) & at_pole).astype(jnp.int32))[..., 0]
    rolled = halo_in(fields, 4)
    rolled_cot = halo_in(cotangent, 2)
    window_in = to_windows(rolled.astype(jnp.float32))
    normed, norm_back = jax.vjp(norm_rows, window_in)
    qkv = jnp.dot(normed, qkv_weight, preferred_element_type=jnp.float32)
    attended, attend_back = jax.vjp(lambda inner: attend(inner, region), qkv)
    proj = jnp.dot(attended, out_weight, preferred_element_type=jnp.float32)
    proj = from_windows(proj, height, breadth, levels)
    block = (rolled.astype(jnp.float32) + proj).astype(jnp.bfloat16)
    normed4, norm4_back = jax.vjp(norm_rows, merge_cells(block.astype(jnp.float32)))
    merged = jnp.dot(normed4, merge_weight, preferred_element_type=jnp.float32).astype(jnp.bfloat16)
    merge_term = token_sum(normed4, rolled_cot)
    d_normed4 = back_product(rolled_cot, merge_weight).astype(jnp.bfloat16)
    d_block = split_cells(norm4_back(d_normed4)[0]).astype(jnp.bfloat16)
    d_proj = to_windows(d_block)
    out_term = token_sum(attended, d_proj)
    d_attended = back_product(d_proj, out_weight).astype(jnp.bfloat16)
    d_qkv = attend_back(d_attended)[0].astype(jnp.bfloat16)
    qkv_term = token_sum(normed, d_qkv)
    d_normed = back_product(d_qkv, qkv_weight).astype(jnp.bfloat16)
    d_window = norm_back(d_normed)[0]
    d_rolled = from_windows(d_window, height, breadth, levels)
    field_grad = (d_block.astype(jnp.float32) + d_rolled).astype(jnp.bfloat16)
    merged = halo_out(merged, 2)
    field_grad = halo_out(field_grad, 4)

    m = merge_term.reshape(4, 2, 4, 2, 2, 16, 4, 256).transpose(3, 4, 2, 0, 1, 6, 5, 7)
    q = jnp.concatenate([qkv_term.reshape(512, 4, 384), out_term.reshape(512, 4, 128)], axis=-1)
    q = q.reshape(4, 2, 4, 2, 8, 4, 2, 256).transpose(3, 6, 2, 0, 1, 5, 4, 7)

    def reduce(t):
        t = scatter_sum(t, "c")
        one, two = t[0], jnp.swapaxes(t[1], 0, 1)
        one, two = scatter_sum(one, "x"), scatter_sum(two, "y")
        one, two = scatter_sum(one, "y"), scatter_sum(two, "x")
        both = jnp.concatenate([one, two], axis=-2)
        return scatter_sum(both.reshape(8, *both.shape[2:]), Z)

    merge_grad = reduce(m)
    rest = reduce(q)
    rest = jnp.concatenate([rest[:8], rest[8:]], axis=-1)
    qkv_grad, out_grad = rest[:, :384], rest[:, 384:]
    return (merged, field_grad, qkv_grad, out_grad, merge_grad)


def solution(mesh):
    fine = Mesh(mesh.devices.reshape(4, 2, 4, 2, 4), ALL)
    tokens = P(LAT, "zl", None, None)
    grads = P(LAT, "zl")
    return jax.shard_map(
        local,
        mesh=fine,
        in_specs=(tokens, P(), P(), P(), tokens),
        out_specs=(tokens, tokens, grads, grads, grads),
        check_vma=False,
    )
```

```python
import functools

import numpy as np
import jax
import jax.numpy as jnp
from jax import lax
from jax.experimental import pallas as pl
from jax.experimental.pallas import tpu as pltpu
from jax.sharding import Mesh, PartitionSpec as P

LAT = ("y", "zh", "x", "c")
ALL = ("y", "zh", "x", "c", "zl")
Z = ("zh", "zl")
YX = ("y", "x")
XC = ("x", "c")
F32 = jnp.float32
BF16 = jnp.bfloat16
D = 512
EPS = 1e-5
LIMIT = 60 * 1024 * 1024


def dot(a, b):
    return lax.dot_general(a, b, (((1,), (0,)), ((), ())), preferred_element_type=F32)


def dot_nt(a, b):
    return lax.dot_general(a, b, (((1,), (1,)), ((), ())), preferred_element_type=F32)


def dot_tn(a, b):
    return lax.dot_general(a, b, (((0,), (0,)), ((), ())), preferred_element_type=F32)


def stack_heads(t):
    lane = lax.broadcasted_iota(jnp.int32, t.shape, 1)
    zero = jnp.zeros_like(t)
    return jnp.concatenate([jnp.where(lane < 64, t, zero), jnp.where(lane < 64, zero, t)], axis=0)


def side_by_side(t):
    return jnp.concatenate([t[:128], t[128:]], axis=1)


def copies(pairs, sems):
    return [pltpu.make_async_copy(src, dst, sems.at[i]) for i, (src, dst) in enumerate(pairs)]


def forward_kernel(
    info_ref, top_ref, bottom_ref, cot_ref, wqkv_hbm, wout_hbm, wm_hbm,
    x_hbm, normed_hbm, qkv_hbm, probs_hbm, att_hbm, dblock_hbm, n4t_hbm, merged_ref,
    wqkv_ref, wout_ref, wm_ref, x_ref, normed_ref, qkv_ref, probs_ref, att_ref, dblock_ref, n4t_ref,
    block_ref, dn4_ref, in_sems, out_sems,
):
    loads = copies([(wqkv_hbm, wqkv_ref), (wout_hbm, wout_ref), (wm_hbm, wm_ref)], in_sems)
    x_out, normed_out, qkv_out, probs_out, att_out, dblock_out, n4t_out = stores = copies(
        [
            (x_ref, x_hbm), (normed_ref, normed_hbm), (qkv_ref, qkv_hbm), (probs_ref, probs_hbm),
            (att_ref, att_hbm), (dblock_ref, dblock_hbm), (n4t_ref, n4t_hbm),
        ],
        out_sems,
    )
    for load in loads:
        load.start()
    at_pole = info_ref[0]
    x_ref[:, :, :16] = top_ref[...]
    x_ref[:, :, 16:] = bottom_ref[...]
    x_out.start()

    @pl.loop(0, 4)
    def _(w):
        x = x_ref[w].reshape(128, D).astype(F32)
        c = x - jnp.mean(x, axis=-1, keepdims=True)
        r = lax.rsqrt(jnp.mean(c * c, axis=-1, keepdims=True) + EPS)
        normed_ref[pl.ds(w * 128, 128), :] = (c * r).astype(BF16)

    normed_out.start()
    loads[0].wait()
    for n in range(6):
        cols = slice(n * 256, n * 256 + 256)
        t = dot(normed_ref[...], wqkv_ref[:, cols])
        if n < 2:
            t = t * 0.125
        qkv_ref[:, cols] = t.astype(BF16)
    qkv_out.start()

    row_q = lax.broadcasted_iota(jnp.int32, (256, 128), 0) % 32 // 16
    row_k = lax.broadcasted_iota(jnp.int32, (256, 128), 1) % 32 // 16
    allowed = (row_q == row_k) | (at_pole == 0)

    @pl.loop(0, 4)
    def _(w):
        rows = pl.ds(w * 128, 128)
        for p in range(4):
            q = qkv_ref[rows, p * 128 : p * 128 + 128]
            k = qkv_ref[rows, 512 + p * 128 : 512 + p * 128 + 128]
            v = qkv_ref[rows, 1024 + p * 128 : 1024 + p * 128 + 128]
            s = jnp.where(allowed, dot_nt(stack_heads(q), k), -1e9)
            e = jnp.exp(s - jnp.max(s, axis=-1, keepdims=True))
            probs = e / jnp.sum(e, axis=-1, keepdims=True)
            probs_ref[w, p] = probs
            o = dot(side_by_side(probs.astype(BF16)), stack_heads(v))
            att_ref[rows, p * 128 : p * 128 + 128] = o.astype(BF16)

    probs_out.start()
    att_out.start()
    loads[1].wait()
    for n in range(2):
        cols = slice(n * 256, n * 256 + 256)
        proj = dot(att_ref[...], wout_ref[:, cols]).reshape(4, 4, 32, 256)
        block_ref[:, :, :, cols] = (x_ref[:, :, :, cols].astype(F32) + proj).astype(BF16)

    loads[2].wait()
    for q in range(4):
        for n in range(2):
            cols = slice(q * D + n * 256, q * D + n * 256 + 256)
            dn4_ref[:, cols] = dot_nt(cot_ref[...], wm_ref[cols, :]).astype(BF16)

    def cell(q):
        return block_ref[:, q].reshape(128, D).astype(F32)

    total = jnp.zeros((128, 1), F32)
    for q in range(4):
        total = total + jnp.sum(cell(q), axis=-1, keepdims=True)
    mean = total * (1.0 / 2048)
    total = jnp.zeros((128, 1), F32)
    for q in range(4):
        c = cell(q) - mean
        total = total + jnp.sum(c * c, axis=-1, keepdims=True)
    r = lax.rsqrt(total * (1.0 / 2048) + EPS)
    merged = jnp.zeros((128, 1024), F32)
    m1 = jnp.zeros((128, 1), F32)
    m2 = jnp.zeros((128, 1), F32)
    for q in range(4):
        y = (cell(q) - mean) * r
        dy = dn4_ref[:, q * D : q * D + D].astype(F32)
        m1 = m1 + jnp.sum(dy, axis=-1, keepdims=True)
        m2 = m2 + jnp.sum(dy * y, axis=-1, keepdims=True)
        yb = y.astype(BF16)
        t = yb.T.reshape(2, 8, 32, 128)
        for zh in range(2):
            n4t_ref[:, q, zh] = t[zh]
        merged = merged + dot(yb, wm_ref[q * D : q * D + D, :])
    n4t_out.start()
    merged_ref[...] = merged.astype(BF16)
    m1 = m1 * (1.0 / 2048)
    m2 = m2 * (1.0 / 2048)
    for q in range(4):
        y = (cell(q) - mean) * r
        dy = dn4_ref[:, q * D : q * D + D].astype(F32)
        dblock_ref[:, q] = (r * (dy - m1 - y * m2)).astype(BF16).reshape(4, 32, D)
    dblock_out.start()
    for store in stores:
        store.wait()


def backward_kernel(
    info_ref, normed_hbm, qkv_hbm, probs_hbm, att_hbm, dblock_hbm, wout_hbm,
    dqkv_hbm, keep_hbm, send_hbm,
    datt_ref, term_ref, t_ref, normed_ref, qkv_ref, probs_ref, att_ref, dblock_ref, wout_ref, dqkv_ref,
    in_sems, out_sems, term_sems,
):
    core = info_ref[1]
    loads = copies(
        [
            (dblock_hbm, dblock_ref), (att_hbm, att_ref), (wout_hbm, wout_ref), (qkv_hbm, qkv_ref),
            (probs_hbm, probs_ref), (normed_hbm, normed_ref),
        ],
        in_sems,
    )
    stores = []

    def add_term(n, value):
        cols = slice(n * 256, n * 256 + 256)
        value = value.reshape(32, 2, 8, 256)
        for y in range(4):
            for zh in range(2):
                g = (y * 2 + zh) * 4
                for c in range(2):
                    term_ref[c, y, :, zh, :, cols] = value[g : g + 4, c]
        for i, (c, hbm) in enumerate(((core, keep_hbm), (1 - core, send_hbm))):
            store = pltpu.make_async_copy(
                term_ref.at[c, :, :, :, :, cols], hbm.at[:, :, :, :, cols], term_sems.at[2 * n + i]
            )
            store.start()
            stores.append(store)

    for load in loads:
        load.start()
    loads[0].wait()
    loads[1].wait()
    t_ref[...] = att_ref[...].T
    for n in range(2):
        cols = slice(n * 256, n * 256 + 256)
        add_term(6 + n, dot(t_ref[...], dblock_ref[:, :, :, cols].reshape(512, 256)))
    loads[2].wait()
    for n in range(2):
        cols = slice(n * 256, n * 256 + 256)
        datt_ref[:, cols] = dot_nt(dblock_ref[...].reshape(512, D), wout_ref[cols, :]).astype(BF16)
    loads[3].wait()
    loads[4].wait()

    @pl.loop(0, 4)
    def _(w):
        rows = pl.ds(w * 128, 128)
        for p in range(4):
            q = stack_heads(qkv_ref[rows, p * 128 : p * 128 + 128])
            k = stack_heads(qkv_ref[rows, 512 + p * 128 : 512 + p * 128 + 128])
            v = qkv_ref[rows, 1024 + p * 128 : 1024 + p * 128 + 128]
            do = stack_heads(datt_ref[rows, p * 128 : p * 128 + 128])
            probs = probs_ref[w, p]
            dp = dot_nt(do, v).astype(BF16).astype(F32)
            ds = (probs * (dp - jnp.sum(probs * dp, axis=-1, keepdims=True))).astype(BF16)
            dq = dot(side_by_side(ds), k) * 0.125
            dk = dot_tn(ds, q)
            dv = dot_tn(probs.astype(BF16), do)
            dqkv_ref[rows, p * 128 : p * 128 + 128] = dq.astype(BF16)
            dqkv_ref[rows, 512 + p * 128 : 512 + p * 128 + 128] = dk.astype(BF16)
            dqkv_ref[rows, 1024 + p * 128 : 1024 + p * 128 + 128] = dv.astype(BF16)

    (dqkv_out,) = copies([(dqkv_ref, dqkv_hbm)], out_sems)
    dqkv_out.start()
    loads[5].wait()
    t_ref[...] = normed_ref[...].T
    for n in range(6):
        add_term(n, dot(t_ref[...], dqkv_ref[:, n * 256 : n * 256 + 256]))
    dqkv_out.wait()
    for store in stores:
        store.wait()


def last_kernel(
    info_ref, n4t_hbm, mine_hbm, theirs_hbm, x_hbm, dblock_hbm, dqkv_hbm, wqkv_hbm,
    keep_ref, s1_ref, s2_ref, s3_ref, out_ref,
    t_ref, dn_ref, n4t_ref, mine_ref, theirs_ref, x_ref, dblock_ref, dqkv_ref, wqkv_ref, in_sems,
):
    loads = copies(
        [
            (n4t_hbm, n4t_ref), (mine_hbm, mine_ref), (theirs_hbm, theirs_ref), (dqkv_hbm, dqkv_ref),
            (wqkv_hbm, wqkv_ref), (x_hbm, x_ref), (dblock_hbm, dblock_ref),
        ],
        in_sems,
    )
    for load in loads:
        load.start()
    for load in loads[:3]:
        load.wait()
    core, y_mine, x_mine = info_ref[1], info_ref[2], info_ref[3]
    source = [lax.rem(x_mine + 4 - k, 4) * 2 + c for c in (core, 1 - core) for k in range(4)]
    for n in range(2):
        cols = slice(n * 512, n * 512 + 512)
        right = jnp.concatenate([r[:, :, cols].reshape(512, 512) for r in (mine_ref, theirs_ref)], axis=0)
        for y in range(4):
            left = jnp.concatenate([n4t_ref[s, y].reshape(64, 128) for s in source], axis=1)
            t_ref[y, :, cols] = dot(left, right)
    keep_ref[...] = t_ref[y_mine]
    for by, ref in ((1, s1_ref), (2, s2_ref), (3, s3_ref)):
        ref[...] = t_ref[lax.rem(y_mine + by, 4)].astype(BF16)

    for load in loads[3:]:
        load.wait()
    for n in range(2):
        cols = slice(n * 256, n * 256 + 256)
        dn_ref[:, cols] = dot_nt(dqkv_ref[...], wqkv_ref[cols, :]).astype(BF16)

    @pl.loop(0, 4)
    def _(w):
        x = x_ref[w].reshape(128, D).astype(F32)
        c = x - jnp.mean(x, axis=-1, keepdims=True)
        r = lax.rsqrt(jnp.mean(c * c, axis=-1, keepdims=True) + EPS)
        y = c * r
        dy = dn_ref[pl.ds(w * 128, 128), :].astype(F32)
        m1 = jnp.mean(dy, axis=-1, keepdims=True)
        m2 = jnp.mean(dy * y, axis=-1, keepdims=True)
        dx = r * (dy - m1 - y * m2)
        out_ref[w] = (dblock_ref[w].reshape(128, D).astype(F32) + dx).astype(BF16).reshape(4, 32, D)


def ring(axes, by):
    count = lax.axis_size(axes)
    return [(i, (i + by) % count) for i in range(count)]


def diagonal(by):
    lats, lons = lax.axis_size(LAT), lax.axis_size("zl")
    return [
        (i * lons + j, (i + by) % lats * lons + (j + by) % lons)
        for i in range(lats)
        for j in range(lons)
    ]


def as_fields(t):
    r, n = t.shape[:2]
    return t.reshape(r, n, 2, 2, D).transpose(0, 1, 3, 2, 4).reshape(r, 2 * n, 2, D)


def as_merged(t):
    r, n = t.shape[:2]
    return t.reshape(r, n // 2, 2, 2, D).transpose(0, 1, 3, 2, 4).reshape(r, n // 2, 2, 2 * D)


def pack(f, m):
    return jnp.concatenate([f, as_fields(m)], axis=0)


def tokens_of(t):
    return t.reshape(2, 2, 4, 4, 2, 2, D).transpose(2, 4, 1, 0, 3, 5, 6).reshape(4, 4, 16, D)


def halo_in(f, m):
    first, f, m = lax.optimization_barrier((f[:4, 4:], f, m))
    f_below = lax.ppermute(first, LAT, ring(LAT, -1))
    second, f, m = lax.optimization_barrier((m[:2, 2:], f, m))
    m_below = lax.ppermute(second, LAT, ring(LAT, -1))
    corner = lax.ppermute(pack(f[:4, :4], m[:2, :2]), ALL, diagonal(-1))
    right = lax.ppermute(pack(f[4:, :4], m[2:, :2]), "zl", ring("zl", -1))
    top = tokens_of(jnp.concatenate([f[4:, 4:], right[:4]], axis=1))
    bottom = tokens_of(jnp.concatenate([f_below, corner[:4]], axis=1))
    m_top = jnp.concatenate([m[2:, 2:], as_merged(right[4:])], axis=1)
    m_bottom = jnp.concatenate([m_below, as_merged(corner[4:])], axis=1)
    return top, bottom, jnp.concatenate([m_top, m_bottom], axis=0)


def halo_out(t, h):
    w = t.shape[1] - h
    first, t = lax.optimization_barrier((t[h:, :w], t))
    above = lax.ppermute(first, LAT, ring(LAT, 1))
    corner = lax.ppermute(t[h:, w:], ALL, diagonal(1))
    left = lax.ppermute(t[:h, w:], "zl", ring("zl", 1))
    top = jnp.concatenate([corner, above], axis=1)
    bottom = jnp.concatenate([left, t[:h, :w]], axis=1)
    return jnp.concatenate([top, bottom], axis=0)


def swap_cores(t):
    return lax.ppermute(t, "c", [(0, 1), (1, 0)])


def call(kernel, outs, scratch, flops, *args):
    smem = pl.BlockSpec(memory_space=pltpu.SMEM)
    vmem = pl.BlockSpec(memory_space=pltpu.VMEM)
    hbm = pl.BlockSpec(memory_space=pl.ANY)
    args = [a if isinstance(a, tuple) else (a, False) for a in args]
    return pl.pallas_call(
        kernel,
        out_shape=[jax.ShapeDtypeStruct(shape, dtype) for shape, dtype, _ in outs],
        in_specs=[smem if a.dtype == jnp.int32 else hbm if far else vmem for a, far in args],
        out_specs=[hbm if far else vmem for _, _, far in outs],
        scratch_shapes=[pltpu.SemaphoreType.DMA((t,)) if isinstance(t, int) else pltpu.VMEM(*t) for t in scratch],
        compiler_params=pltpu.CompilerParams(vmem_limit_bytes=LIMIT),
        cost_estimate=pl.CostEstimate(flops=flops, bytes_accessed=1000, transcendentals=0),
    )(*[a for a, _ in args])


def local(fields, qkv_weight, out_weight, merge_weight, cotangent):
    pole = (lax.axis_index(LAT) == lax.axis_size(LAT) - 1).astype(jnp.int32)
    info = jnp.stack([pole] + [lax.axis_index(axis).astype(jnp.int32) for axis in ("c", "y", "x")])
    top, bottom, rolled_cot = halo_in(fields, cotangent)
    cot = rolled_cot.reshape(4, 4, 4, 2, 1024).transpose(1, 0, 2, 3, 4).reshape(128, 1024)
    cells, square = ((4, 4, 32, D), BF16), ((512, 512), BF16)
    wide, probabilities, quarters = ((512, 1536), BF16), ((4, 4, 256, 128), F32), ((8, 4, 2, 32, 128), BF16)
    kept = [cells, square, wide, probabilities, square, cells, quarters]
    x, normed, qkv, probs, att, d_block, n4t, merged = call(
        forward_kernel,
        [(*t, True) for t in kept] + [((128, 1024), BF16, False)],
        [wide, square, ((2048, 1024), BF16), *kept, cells, ((128, 2048), BF16), 3, 7],
        15000000000,
        info, top, bottom, cot, (qkv_weight, True), (out_weight, True), (merge_weight, True),
    )
    cot, d_block = lax.optimization_barrier((cot, d_block))
    cot_mine = jnp.stack([cot] + [lax.ppermute(cot, "x", ring("x", by)) for by in (1, 2, 3)])
    cot_theirs = swap_cores(cot_mine)
    n4t = lax.all_to_all(n4t, XC, 0, 0)
    merged = merged.reshape(4, 4, 4, 2, 1024).transpose(1, 0, 2, 3, 4).reshape(4, 16, 2, 1024)
    part = ((4, 4, 2, 8, 2048), F32, True)
    d_qkv, term_keep, term_send = call(
        backward_kernel,
        [(*wide, True), part, part],
        [square, ((2, 4, 4, 2, 8, 2048), F32), square, square, wide, probabilities, square, cells, square, wide, 6, 1, 16],
        12800000000,
        info, *((t, True) for t in (normed, qkv, probs, att, d_block, out_weight)),
    )
    term_send, n4t, cot_theirs = lax.optimization_barrier((term_send, n4t, cot_theirs))
    term = (term_keep + swap_cores(term_send)).astype(BF16).reshape(16, 2, 8, 2048)
    term, d_qkv, n4t, merged = lax.optimization_barrier((term, d_qkv, n4t, merged))
    term_got = lax.all_to_all(term, YX, 0, 0)
    group = ((4, 128, 1024), BF16)
    m, s1, s2, s3, field_grad = call(
        last_kernel,
        [((64, 1024), F32, False)] + [((64, 1024), BF16, False)] * 3 + [(*cells, False)],
        [((4, 64, 1024), F32), square, quarters, group, group, cells, cells, wide, wide, 7],
        1000000,
        info, *((t, True) for t in (n4t, cot_mine, cot_theirs, x, d_block, d_qkv, qkv_weight)),
    )
    for by, piece in ((1, s1), (2, s2), (3, s3)):
        m = m + lax.ppermute(piece, "y", ring("y", by)).astype(F32)
    field_grad = field_grad.reshape(4, 2, 2, 4, 4, 2, D).transpose(3, 2, 0, 4, 1, 5, 6).reshape(8, 32, 2, D)
    field_grad = halo_out(field_grad, 4)
    merged = halo_out(merged, 2)
    term_got, m, merged = lax.optimization_barrier((term_got, m, merged))

    m = m.reshape(2, 32, 4, 256).transpose(0, 2, 1, 3).reshape(8, 32, 256)
    q = jnp.sum(term_got.astype(F32), axis=0)
    qa = q[..., :1536].reshape(2, 8, 4, 384).transpose(0, 2, 1, 3)
    qb = q[..., 1536:].reshape(2, 8, 4, 128).transpose(0, 2, 1, 3)
    q = jnp.concatenate([qa[..., :256], jnp.concatenate([qa[..., 256:], qb], axis=-1)], axis=2).reshape(8, 16, 256)
    both = jnp.concatenate([m, q], axis=1)
    both = jnp.sum(lax.all_to_all(both, Z, 0, 0), axis=0)
    merge_grad = both[:32]
    qkv_grad = jnp.concatenate([both[32:40], both[40:48, :128]], axis=-1)
    out_grad = both[40:48, 128:]
    return (merged, field_grad, qkv_grad, out_grad, merge_grad)


def solution(mesh):
    fine = Mesh(mesh.devices.reshape(4, 2, 4, 2, 4), ALL)
    tokens = P(LAT, "zl", None, None)
    grads = P(LAT, "zl")
    return jax.shard_map(
        local,
        mesh=fine,
        in_specs=(tokens, P(), P(), P(), tokens),
        out_specs=(tokens, tokens, grads, grads, grads),
        check_vma=False,
    )
```

```python
import functools

import numpy as np
import jax
import jax.numpy as jnp
from jax import lax
from jax.experimental import pallas as pl
from jax.experimental.pallas import tpu as pltpu
from jax.sharding import Mesh, PartitionSpec as P

LAT = ("y", "zh", "x", "c")
ALL = ("y", "zh", "x", "c", "zl")
Z = ("zh", "zl")
YX = ("y", "x")
XC = ("x", "c")
F32 = jnp.float32
BF16 = jnp.bfloat16
D = 512
EPS = 1e-5
LIMIT = 60 * 1024 * 1024


def dot(a, b):
    return lax.dot_general(a, b, (((1,), (0,)), ((), ())), preferred_element_type=F32)


def dot_nt(a, b):
    return lax.dot_general(a, b, (((1,), (1,)), ((), ())), preferred_element_type=F32)


def dot_tn(a, b):
    return lax.dot_general(a, b, (((0,), (0,)), ((), ())), preferred_element_type=F32)


def stack_heads(t):
    lane = lax.broadcasted_iota(jnp.int32, t.shape, 1)
    zero = jnp.zeros_like(t)
    return jnp.concatenate([jnp.where(lane < 64, t, zero), jnp.where(lane < 64, zero, t)], axis=0)


def side_by_side(t):
    return jnp.concatenate([t[:128], t[128:]], axis=1)


def copies(pairs, sems):
    return [pltpu.make_async_copy(src, dst, sems.at[i]) for i, (src, dst) in enumerate(pairs)]


def forward_kernel(
    info_ref, top_ref, bottom_ref, cot_ref, wqkv_hbm, wout_hbm, wm_hbm,
    x_hbm, normed_hbm, qkv_hbm, probs_hbm, att_hbm, dblock_hbm, n4t_hbm, merged_ref,
    wqkv_ref, wout_ref, wm_ref, x_ref, normed_ref, qkv_ref, probs_ref, att_ref, dblock_ref, n4t_ref,
    block_ref, dn4_ref, in_sems, out_sems,
):
    loads = copies([(wqkv_hbm, wqkv_ref), (wout_hbm, wout_ref), (wm_hbm, wm_ref)], in_sems)
    x_out, normed_out, qkv_out, probs_out, att_out, dblock_out, n4t_out = stores = copies(
        [
            (x_ref, x_hbm), (normed_ref, normed_hbm), (qkv_ref, qkv_hbm), (probs_ref, probs_hbm),
            (att_ref, att_hbm), (dblock_ref, dblock_hbm), (n4t_ref, n4t_hbm),
        ],
        out_sems,
    )
    for load in loads:
        load.start()
    at_pole = info_ref[0]
    x_ref[:, :, :16] = top_ref[...]
    x_ref[:, :, 16:] = bottom_ref[...]
    x_out.start()

    @pl.loop(0, 4)
    def _(w):
        x = x_ref[w].reshape(128, D).astype(F32)
        c = x - jnp.mean(x, axis=-1, keepdims=True)
        r = lax.rsqrt(jnp.mean(c * c, axis=-1, keepdims=True) + EPS)
        normed_ref[pl.ds(w * 128, 128), :] = (c * r).astype(BF16)

    normed_out.start()
    loads[0].wait()
    for n in range(6):
        cols = slice(n * 256, n * 256 + 256)
        t = dot(normed_ref[...], wqkv_ref[:, cols])
        if n < 2:
            t = t * 0.125
        qkv_ref[:, cols] = t.astype(BF16)
    qkv_out.start()

    row_q = lax.broadcasted_iota(jnp.int32, (256, 128), 0) % 32 // 16
    row_k = lax.broadcasted_iota(jnp.int32, (256, 128), 1) % 32 // 16
    allowed = (row_q == row_k) | (at_pole == 0)

    @pl.loop(0, 4)
    def _(w):
        rows = pl.ds(w * 128, 128)
        for p in range(4):
            q = qkv_ref[rows, p * 128 : p * 128 + 128]
            k = qkv_ref[rows, 512 + p * 128 : 512 + p * 128 + 128]
            v = qkv_ref[rows, 1024 + p * 128 : 1024 + p * 128 + 128]
            s = jnp.where(allowed, dot_nt(stack_heads(q), k), -1e9)
            e = jnp.exp(s - jnp.max(s, axis=-1, keepdims=True))
            probs = e / jnp.sum(e, axis=-1, keepdims=True)
            probs_ref[w, p] = probs
            o = dot(side_by_side(probs.astype(BF16)), stack_heads(v))
            att_ref[rows, p * 128 : p * 128 + 128] = o.astype(BF16)

    probs_out.start()
    att_out.start()
    loads[1].wait()
    for n in range(2):
        cols = slice(n * 256, n * 256 + 256)
        proj = dot(att_ref[...], wout_ref[:, cols]).reshape(4, 4, 32, 256)
        block_ref[:, :, :, cols] = (x_ref[:, :, :, cols].astype(F32) + proj).astype(BF16)

    loads[2].wait()
    for q in range(4):
        for n in range(2):
            cols = slice(q * D + n * 256, q * D + n * 256 + 256)
            dn4_ref[:, cols] = dot_nt(cot_ref[...], wm_ref[cols, :]).astype(BF16)

    def cell(q):
        return block_ref[:, q].reshape(128, D).astype(F32)

    total = jnp.zeros((128, 1), F32)
    for q in range(4):
        total = total + jnp.sum(cell(q), axis=-1, keepdims=True)
    mean = total * (1.0 / 2048)
    total = jnp.zeros((128, 1), F32)
    for q in range(4):
        c = cell(q) - mean
        total = total + jnp.sum(c * c, axis=-1, keepdims=True)
    r = lax.rsqrt(total * (1.0 / 2048) + EPS)
    merged = jnp.zeros((128, 1024), F32)
    m1 = jnp.zeros((128, 1), F32)
    m2 = jnp.zeros((128, 1), F32)
    for q in range(4):
        y = (cell(q) - mean) * r
        dy = dn4_ref[:, q * D : q * D + D].astype(F32)
        m1 = m1 + jnp.sum(dy, axis=-1, keepdims=True)
        m2 = m2 + jnp.sum(dy * y, axis=-1, keepdims=True)
        yb = y.astype(BF16)
        t = yb.T.reshape(2, 8, 32, 128)
        for zh in range(2):
            n4t_ref[:, q, zh] = t[zh]
        merged = merged + dot(yb, wm_ref[q * D : q * D + D, :])
    n4t_out.start()
    merged_ref[...] = merged.astype(BF16)
    m1 = m1 * (1.0 / 2048)
    m2 = m2 * (1.0 / 2048)
    for q in range(4):
        y = (cell(q) - mean) * r
        dy = dn4_ref[:, q * D : q * D + D].astype(F32)
        dblock_ref[:, q] = (r * (dy - m1 - y * m2)).astype(BF16).reshape(4, 32, D)
    dblock_out.start()
    for store in stores:
        store.wait()


def backward_kernel(
    info_ref, normed_hbm, qkv_hbm, probs_hbm, att_hbm, dblock_hbm, wout_hbm,
    dqkv_hbm, keep_hbm, send_hbm,
    datt_ref, term_ref, t_ref, normed_ref, qkv_ref, probs_ref, att_ref, dblock_ref, wout_ref, dqkv_ref,
    in_sems, out_sems, term_sems,
):
    core = info_ref[1]
    loads = copies(
        [
            (dblock_hbm, dblock_ref), (att_hbm, att_ref), (wout_hbm, wout_ref), (qkv_hbm, qkv_ref),
            (probs_hbm, probs_ref), (normed_hbm, normed_ref),
        ],
        in_sems,
    )
    stores = []

    def add_term(n, value):
        cols = slice(n * 256, n * 256 + 256)
        value = value.reshape(32, 2, 8, 256)
        for y in range(4):
            for zh in range(2):
                g = (y * 2 + zh) * 4
                for c in range(2):
                    term_ref[c, y, :, zh, :, cols] = value[g : g + 4, c]
        for i, (c, hbm) in enumerate(((core, keep_hbm), (1 - core, send_hbm))):
            store = pltpu.make_async_copy(
                term_ref.at[c, :, :, :, :, cols], hbm.at[:, :, :, :, cols], term_sems.at[2 * n + i]
            )
            store.start()
            stores.append(store)

    for load in loads:
        load.start()
    loads[0].wait()
    loads[1].wait()
    t_ref[...] = att_ref[...].T
    for n in range(2):
        cols = slice(n * 256, n * 256 + 256)
        add_term(6 + n, dot(t_ref[...], dblock_ref[:, :, :, cols].reshape(512, 256)))
    loads[2].wait()
    for n in range(2):
        cols = slice(n * 256, n * 256 + 256)
        datt_ref[:, cols] = dot_nt(dblock_ref[...].reshape(512, D), wout_ref[cols, :]).astype(BF16)
    loads[3].wait()
    loads[4].wait()

    @pl.loop(0, 4)
    def _(w):
        rows = pl.ds(w * 128, 128)
        for p in range(4):
            q = stack_heads(qkv_ref[rows, p * 128 : p * 128 + 128])
            k = stack_heads(qkv_ref[rows, 512 + p * 128 : 512 + p * 128 + 128])
            v = qkv_ref[rows, 1024 + p * 128 : 1024 + p * 128 + 128]
            do = stack_heads(datt_ref[rows, p * 128 : p * 128 + 128])
            probs = probs_ref[w, p]
            dp = dot_nt(do, v).astype(BF16).astype(F32)
            ds = (probs * (dp - jnp.sum(probs * dp, axis=-1, keepdims=True))).astype(BF16)
            dq = dot(side_by_side(ds), k) * 0.125
            dk = dot_tn(ds, q)
            dv = dot_tn(probs.astype(BF16), do)
            dqkv_ref[rows, p * 128 : p * 128 + 128] = dq.astype(BF16)
            dqkv_ref[rows, 512 + p * 128 : 512 + p * 128 + 128] = dk.astype(BF16)
            dqkv_ref[rows, 1024 + p * 128 : 1024 + p * 128 + 128] = dv.astype(BF16)

    (dqkv_out,) = copies([(dqkv_ref, dqkv_hbm)], out_sems)
    dqkv_out.start()
    loads[5].wait()
    t_ref[...] = normed_ref[...].T
    for n in range(6):
        add_term(n, dot(t_ref[...], dqkv_ref[:, n * 256 : n * 256 + 256]))
    dqkv_out.wait()
    for store in stores:
        store.wait()


def last_kernel(
    info_ref, n4t_hbm, mine_hbm, theirs_hbm, x_hbm, dblock_hbm, dqkv_hbm, wqkv_hbm,
    keep_ref, s1_ref, s2_ref, s3_ref, out_ref,
    t_ref, dn_ref, n4t_ref, mine_ref, theirs_ref, x_ref, dblock_ref, dqkv_ref, wqkv_ref, in_sems,
):
    loads = copies(
        [
            (n4t_hbm, n4t_ref), (mine_hbm, mine_ref), (theirs_hbm, theirs_ref), (dqkv_hbm, dqkv_ref),
            (wqkv_hbm, wqkv_ref), (x_hbm, x_ref), (dblock_hbm, dblock_ref),
        ],
        in_sems,
    )
    for load in loads:
        load.start()
    for load in loads[:3]:
        load.wait()
    core, y_mine, x_mine = info_ref[1], info_ref[2], info_ref[3]
    source = [lax.rem(x_mine + 4 - k, 4) * 2 + c for c in (core, 1 - core) for k in range(4)]
    for n in range(2):
        cols = slice(n * 512, n * 512 + 512)
        right = jnp.concatenate([r[:, :, cols].reshape(512, 512) for r in (mine_ref, theirs_ref)], axis=0)
        for y in range(4):
            left = jnp.concatenate([n4t_ref[s, y].reshape(64, 128) for s in source], axis=1)
            t_ref[y, :, cols] = dot(left, right)
    keep_ref[...] = t_ref[y_mine]
    for by, ref in ((1, s1_ref), (2, s2_ref), (3, s3_ref)):
        ref[...] = t_ref[lax.rem(y_mine + by, 4)].astype(BF16)

    for load in loads[3:]:
        load.wait()
    for n in range(2):
        cols = slice(n * 256, n * 256 + 256)
        dn_ref[:, cols] = dot_nt(dqkv_ref[...], wqkv_ref[cols, :]).astype(BF16)

    @pl.loop(0, 4)
    def _(w):
        x = x_ref[w].reshape(128, D).astype(F32)
        c = x - jnp.mean(x, axis=-1, keepdims=True)
        r = lax.rsqrt(jnp.mean(c * c, axis=-1, keepdims=True) + EPS)
        y = c * r
        dy = dn_ref[pl.ds(w * 128, 128), :].astype(F32)
        m1 = jnp.mean(dy, axis=-1, keepdims=True)
        m2 = jnp.mean(dy * y, axis=-1, keepdims=True)
        dx = r * (dy - m1 - y * m2)
        out_ref[w] = (dblock_ref[w].reshape(128, D).astype(F32) + dx).astype(BF16).reshape(4, 32, D)


def ring(axes, by):
    count = lax.axis_size(axes)
    return [(i, (i + by) % count) for i in range(count)]


def diagonal(by):
    lats, lons = lax.axis_size(LAT), lax.axis_size("zl")
    return [
        (i * lons + j, (i + by) % lats * lons + (j + by) % lons)
        for i in range(lats)
        for j in range(lons)
    ]


def as_fields(t):
    r, n = t.shape[:2]
    return t.reshape(r, n, 2, 2, D).transpose(0, 1, 3, 2, 4).reshape(r, 2 * n, 2, D)


def as_merged(t):
    r, n = t.shape[:2]
    return t.reshape(r, n // 2, 2, 2, D).transpose(0, 1, 3, 2, 4).reshape(r, n // 2, 2, 2 * D)


def pack(f, m):
    return jnp.concatenate([f, as_fields(m)], axis=0)


def tokens_of(t):
    return t.reshape(2, 2, 4, 4, 2, 2, D).transpose(2, 4, 1, 0, 3, 5, 6).reshape(4, 4, 16, D)


def halo_in(f, m):
    below, f, m = lax.optimization_barrier((pack(f[:4, 4:], m[:2, 2:]), f, m))
    below = lax.ppermute(below, LAT, ring(LAT, -1))
    corner = lax.ppermute(pack(f[:4, :4], m[:2, :2]), ALL, diagonal(-1))
    right = lax.ppermute(pack(f[4:, :4], m[2:, :2]), "zl", ring("zl", -1))
    top = tokens_of(jnp.concatenate([f[4:, 4:], right[:4]], axis=1))
    bottom = tokens_of(jnp.concatenate([below[:4], corner[:4]], axis=1))
    m_top = jnp.concatenate([m[2:, 2:], as_merged(right[4:])], axis=1)
    m_bottom = jnp.concatenate([as_merged(below[4:]), as_merged(corner[4:])], axis=1)
    return top, bottom, jnp.concatenate([m_top, m_bottom], axis=0)


def halo_out(t, h):
    w = t.shape[1] - h
    first, t = lax.optimization_barrier((t[h:, :w], t))
    above = lax.ppermute(first, LAT, ring(LAT, 1))
    corner = lax.ppermute(t[h:, w:], ALL, diagonal(1))
    left = lax.ppermute(t[:h, w:], "zl", ring("zl", 1))
    top = jnp.concatenate([corner, above], axis=1)
    bottom = jnp.concatenate([left, t[:h, :w]], axis=1)
    return jnp.concatenate([top, bottom], axis=0)


def swap_cores(t):
    return lax.ppermute(t, "c", [(0, 1), (1, 0)])


def call(kernel, outs, scratch, flops, *args):
    smem = pl.BlockSpec(memory_space=pltpu.SMEM)
    vmem = pl.BlockSpec(memory_space=pltpu.VMEM)
    hbm = pl.BlockSpec(memory_space=pl.ANY)
    args = [a if isinstance(a, tuple) else (a, False) for a in args]
    return pl.pallas_call(
        kernel,
        out_shape=[jax.ShapeDtypeStruct(shape, dtype) for shape, dtype, _ in outs],
        in_specs=[smem if a.dtype == jnp.int32 else hbm if far else vmem for a, far in args],
        out_specs=[hbm if far else vmem for _, _, far in outs],
        scratch_shapes=[pltpu.SemaphoreType.DMA((t,)) if isinstance(t, int) else pltpu.VMEM(*t) for t in scratch],
        compiler_params=pltpu.CompilerParams(vmem_limit_bytes=LIMIT),
        cost_estimate=pl.CostEstimate(flops=flops, bytes_accessed=1000, transcendentals=0),
    )(*[a for a, _ in args])


def local(fields, qkv_weight, out_weight, merge_weight, cotangent):
    pole = (lax.axis_index(LAT) == lax.axis_size(LAT) - 1).astype(jnp.int32)
    info = jnp.stack([pole] + [lax.axis_index(axis).astype(jnp.int32) for axis in ("c", "y", "x")])
    top, bottom, rolled_cot = halo_in(fields, cotangent)
    cot = rolled_cot.reshape(4, 4, 4, 2, 1024).transpose(1, 0, 2, 3, 4).reshape(128, 1024)
    cells, square = ((4, 4, 32, D), BF16), ((512, 512), BF16)
    wide, probabilities, quarters = ((512, 1536), BF16), ((4, 4, 256, 128), F32), ((8, 4, 2, 32, 128), BF16)
    kept = [cells, square, wide, probabilities, square, cells, quarters]
    x, normed, qkv, probs, att, d_block, n4t, merged = call(
        forward_kernel,
        [(*t, True) for t in kept] + [((128, 1024), BF16, False)],
        [wide, square, ((2048, 1024), BF16), *kept, cells, ((128, 2048), BF16), 3, 7],
        15000000000,
        info, top, bottom, cot, (qkv_weight, True), (out_weight, True), (merge_weight, True),
    )
    cot, d_block = lax.optimization_barrier((cot, d_block))
    cot_mine = jnp.stack([cot] + [lax.ppermute(cot, "x", ring("x", by)) for by in (1, 2, 3)])
    n4t = lax.all_to_all(n4t, XC, 0, 0)
    merged = merged.reshape(4, 4, 4, 2, 1024).transpose(1, 0, 2, 3, 4).reshape(4, 16, 2, 1024)
    part = ((4, 4, 2, 8, 2048), F32, True)
    d_qkv, term_keep, term_send = call(
        backward_kernel,
        [(*wide, True), part, part],
        [square, ((2, 4, 4, 2, 8, 2048), F32), square, square, wide, probabilities, square, cells, square, wide, 6, 1, 16],
        12800000000,
        info, *((t, True) for t in (normed, qkv, probs, att, d_block, out_weight)),
    )
    term_send, n4t, cot_mine = lax.optimization_barrier((term_send, n4t, cot_mine))
    cot_theirs = swap_cores(cot_mine)
    term = (term_keep + swap_cores(term_send)).astype(BF16).reshape(16, 2, 8, 2048)
    term, d_qkv, n4t, merged = lax.optimization_barrier((term, d_qkv, n4t, merged))
    term_got = lax.all_to_all(term, YX, 0, 0)
    group = ((4, 128, 1024), BF16)
    m, s1, s2, s3, field_grad = call(
        last_kernel,
        [((64, 1024), F32, False)] + [((64, 1024), BF16, False)] * 3 + [(*cells, False)],
        [((4, 64, 1024), F32), square, quarters, group, group, cells, cells, wide, wide, 7],
        1000000,
        info, *((t, True) for t in (n4t, cot_mine, cot_theirs, x, d_block, d_qkv, qkv_weight)),
    )
    for by, piece in ((1, s1), (2, s2), (3, s3)):
        m = m + lax.ppermute(piece, "y", ring("y", by)).astype(F32)
    field_grad = field_grad.reshape(4, 2, 2, 4, 4, 2, D).transpose(3, 2, 0, 4, 1, 5, 6).reshape(8, 32, 2, D)
    field_grad = halo_out(field_grad, 4)
    merged = halo_out(merged, 2)
    term_got, m, field_grad = lax.optimization_barrier((term_got, m, field_grad))

    m = m.reshape(2, 32, 4, 256).transpose(0, 2, 1, 3).reshape(8, 32, 256)
    q = jnp.sum(term_got.astype(F32), axis=0)
    qa = q[..., :1536].reshape(2, 8, 4, 384).transpose(0, 2, 1, 3)
    qb = q[..., 1536:].reshape(2, 8, 4, 128).transpose(0, 2, 1, 3)
    q = jnp.concatenate([qa[..., :256], jnp.concatenate([qa[..., 256:], qb], axis=-1)], axis=2).reshape(8, 16, 256)
    both = jnp.concatenate([m, q], axis=1)
    both = jnp.sum(lax.all_to_all(both, Z, 0, 0), axis=0)
    merge_grad = both[:32]
    qkv_grad = jnp.concatenate([both[32:40], both[40:48, :128]], axis=-1)
    out_grad = both[40:48, 128:]
    return (merged, field_grad, qkv_grad, out_grad, merge_grad)


def solution(mesh):
    fine = Mesh(mesh.devices.reshape(4, 2, 4, 2, 4), ALL)
    tokens = P(LAT, "zl", None, None)
    grads = P(LAT, "zl")
    return jax.shard_map(
        local,
        mesh=fine,
        in_specs=(tokens, P(), P(), P(), tokens),
        out_specs=(tokens, tokens, grads, grads, grads),
        check_vma=False,
    )
```

```python
import functools

import numpy as np
import jax
import jax.numpy as jnp
from jax import lax
from jax.experimental import pallas as pl
from jax.experimental.pallas import tpu as pltpu
from jax.sharding import Mesh, PartitionSpec as P

LAT = ("y", "zh", "x", "c")
ALL = ("y", "zh", "x", "c", "zl")
Z = ("zh", "zl")
YX = ("y", "x")
XC = ("x", "c")
F32 = jnp.float32
BF16 = jnp.bfloat16
D = 512
EPS = 1e-5
LIMIT = 60 * 1024 * 1024


def dot(a, b):
    return lax.dot_general(a, b, (((1,), (0,)), ((), ())), preferred_element_type=F32)


def dot_nt(a, b):
    return lax.dot_general(a, b, (((1,), (1,)), ((), ())), preferred_element_type=F32)


def dot_tn(a, b):
    return lax.dot_general(a, b, (((0,), (0,)), ((), ())), preferred_element_type=F32)


def stack_heads(t):
    lane = lax.broadcasted_iota(jnp.int32, t.shape, 1)
    zero = jnp.zeros_like(t)
    return jnp.concatenate([jnp.where(lane < 64, t, zero), jnp.where(lane < 64, zero, t)], axis=0)


def side_by_side(t):
    return jnp.concatenate([t[:128], t[128:]], axis=1)


def copies(pairs, sems):
    return [pltpu.make_async_copy(src, dst, sems.at[i]) for i, (src, dst) in enumerate(pairs)]


def forward_kernel(
    info_ref, top_ref, bottom_ref, cot_ref, wqkv_hbm, wout_hbm, wm_hbm,
    x_hbm, normed_hbm, qkv_hbm, probs_hbm, att_hbm, dblock_hbm, n4t_hbm, merged_ref,
    wqkv_ref, wout_ref, wm_ref, x_ref, normed_ref, qkv_ref, probs_ref, att_ref, dblock_ref, n4t_ref,
    block_ref, dn4_ref, in_sems, out_sems,
):
    loads = copies([(wqkv_hbm, wqkv_ref), (wout_hbm, wout_ref), (wm_hbm, wm_ref)], in_sems)
    x_out, normed_out, qkv_out, probs_out, att_out, dblock_out, n4t_out = stores = copies(
        [
            (x_ref, x_hbm), (normed_ref, normed_hbm), (qkv_ref, qkv_hbm), (probs_ref, probs_hbm),
            (att_ref, att_hbm), (dblock_ref, dblock_hbm), (n4t_ref, n4t_hbm),
        ],
        out_sems,
    )
    for load in loads:
        load.start()
    at_pole = info_ref[0]
    x_ref[:, :, :16] = top_ref[...]
    x_ref[:, :, 16:] = bottom_ref[...]
    x_out.start()

    @pl.loop(0, 4)
    def _(w):
        x = x_ref[w].reshape(128, D).astype(F32)
        c = x - jnp.mean(x, axis=-1, keepdims=True)
        r = lax.rsqrt(jnp.mean(c * c, axis=-1, keepdims=True) + EPS)
        normed_ref[pl.ds(w * 128, 128), :] = (c * r).astype(BF16)

    normed_out.start()
    loads[0].wait()
    for n in range(6):
        cols = slice(n * 256, n * 256 + 256)
        t = dot(normed_ref[...], wqkv_ref[:, cols])
        if n < 2:
            t = t * 0.125
        qkv_ref[:, cols] = t.astype(BF16)
    qkv_out.start()

    row_q = lax.broadcasted_iota(jnp.int32, (256, 128), 0) % 32 // 16
    row_k = lax.broadcasted_iota(jnp.int32, (256, 128), 1) % 32 // 16
    allowed = (row_q == row_k) | (at_pole == 0)

    @pl.loop(0, 4)
    def _(w):
        rows = pl.ds(w * 128, 128)
        for p in range(4):
            q = qkv_ref[rows, p * 128 : p * 128 + 128]
            k = qkv_ref[rows, 512 + p * 128 : 512 + p * 128 + 128]
            v = qkv_ref[rows, 1024 + p * 128 : 1024 + p * 128 + 128]
            s = jnp.where(allowed, dot_nt(stack_heads(q), k), -1e9)
            e = jnp.exp(s - jnp.max(s, axis=-1, keepdims=True))
            probs = e / jnp.sum(e, axis=-1, keepdims=True)
            probs_ref[w, p] = probs
            o = dot(side_by_side(probs.astype(BF16)), stack_heads(v))
            att_ref[rows, p * 128 : p * 128 + 128] = o.astype(BF16)

    probs_out.start()
    att_out.start()
    loads[1].wait()
    for n in range(2):
        cols = slice(n * 256, n * 256 + 256)
        proj = dot(att_ref[...], wout_ref[:, cols]).reshape(4, 4, 32, 256)
        block_ref[:, :, :, cols] = (x_ref[:, :, :, cols].astype(F32) + proj).astype(BF16)

    loads[2].wait()
    for q in range(4):
        for n in range(2):
            cols = slice(q * D + n * 256, q * D + n * 256 + 256)
            dn4_ref[:, cols] = dot_nt(cot_ref[...], wm_ref[cols, :]).astype(BF16)

    def cell(q):
        return block_ref[:, q].reshape(128, D).astype(F32)

    total = jnp.zeros((128, 1), F32)
    for q in range(4):
        total = total + jnp.sum(cell(q), axis=-1, keepdims=True)
    mean = total * (1.0 / 2048)
    total = jnp.zeros((128, 1), F32)
    for q in range(4):
        c = cell(q) - mean
        total = total + jnp.sum(c * c, axis=-1, keepdims=True)
    r = lax.rsqrt(total * (1.0 / 2048) + EPS)
    merged = jnp.zeros((128, 1024), F32)
    m1 = jnp.zeros((128, 1), F32)
    m2 = jnp.zeros((128, 1), F32)
    for q in range(4):
        y = (cell(q) - mean) * r
        dy = dn4_ref[:, q * D : q * D + D].astype(F32)
        m1 = m1 + jnp.sum(dy, axis=-1, keepdims=True)
        m2 = m2 + jnp.sum(dy * y, axis=-1, keepdims=True)
        yb = y.astype(BF16)
        t = yb.T.reshape(2, 8, 32, 128)
        for zh in range(2):
            n4t_ref[:, q, zh] = t[zh]
        merged = merged + dot(yb, wm_ref[q * D : q * D + D, :])
    n4t_out.start()
    merged_ref[...] = merged.astype(BF16)
    m1 = m1 * (1.0 / 2048)
    m2 = m2 * (1.0 / 2048)
    for q in range(4):
        y = (cell(q) - mean) * r
        dy = dn4_ref[:, q * D : q * D + D].astype(F32)
        dblock_ref[:, q] = (r * (dy - m1 - y * m2)).astype(BF16).reshape(4, 32, D)
    dblock_out.start()
    for store in stores:
        store.wait()


def backward_kernel(
    info_ref, normed_hbm, qkv_hbm, probs_hbm, att_hbm, dblock_hbm, wout_hbm,
    dqkv_hbm, keep_hbm, send_hbm,
    datt_ref, term_ref, t_ref, normed_ref, qkv_ref, probs_ref, att_ref, dblock_ref, wout_ref, dqkv_ref,
    in_sems, out_sems, term_sems,
):
    core = info_ref[1]
    loads = copies(
        [
            (dblock_hbm, dblock_ref), (att_hbm, att_ref), (wout_hbm, wout_ref), (qkv_hbm, qkv_ref),
            (probs_hbm, probs_ref), (normed_hbm, normed_ref),
        ],
        in_sems,
    )
    stores = []

    def add_term(n, value):
        cols = slice(n * 256, n * 256 + 256)
        value = value.reshape(32, 2, 8, 256)
        for y in range(4):
            for zh in range(2):
                g = (y * 2 + zh) * 4
                for c in range(2):
                    term_ref[c, y, :, zh, :, cols] = value[g : g + 4, c]
        for i, (c, hbm) in enumerate(((core, keep_hbm), (1 - core, send_hbm))):
            store = pltpu.make_async_copy(
                term_ref.at[c, :, :, :, :, cols], hbm.at[:, :, :, :, cols], term_sems.at[2 * n + i]
            )
            store.start()
            stores.append(store)

    for load in loads:
        load.start()
    loads[0].wait()
    loads[1].wait()
    t_ref[...] = att_ref[...].T
    for n in range(2):
        cols = slice(n * 256, n * 256 + 256)
        add_term(6 + n, dot(t_ref[...], dblock_ref[:, :, :, cols].reshape(512, 256)))
    loads[2].wait()
    for n in range(2):
        cols = slice(n * 256, n * 256 + 256)
        datt_ref[:, cols] = dot_nt(dblock_ref[...].reshape(512, D), wout_ref[cols, :]).astype(BF16)
    loads[3].wait()
    loads[4].wait()

    @pl.loop(0, 4)
    def _(w):
        rows = pl.ds(w * 128, 128)
        for p in range(4):
            q = stack_heads(qkv_ref[rows, p * 128 : p * 128 + 128])
            k = stack_heads(qkv_ref[rows, 512 + p * 128 : 512 + p * 128 + 128])
            v = qkv_ref[rows, 1024 + p * 128 : 1024 + p * 128 + 128]
            do = stack_heads(datt_ref[rows, p * 128 : p * 128 + 128])
            probs = probs_ref[w, p]
            dp = dot_nt(do, v).astype(BF16).astype(F32)
            ds = (probs * (dp - jnp.sum(probs * dp, axis=-1, keepdims=True))).astype(BF16)
            dq = dot(side_by_side(ds), k) * 0.125
            dk = dot_tn(ds, q)
            dv = dot_tn(probs.astype(BF16), do)
            dqkv_ref[rows, p * 128 : p * 128 + 128] = dq.astype(BF16)
            dqkv_ref[rows, 512 + p * 128 : 512 + p * 128 + 128] = dk.astype(BF16)
            dqkv_ref[rows, 1024 + p * 128 : 1024 + p * 128 + 128] = dv.astype(BF16)

    (dqkv_out,) = copies([(dqkv_ref, dqkv_hbm)], out_sems)
    dqkv_out.start()
    loads[5].wait()
    t_ref[...] = normed_ref[...].T
    for n in range(6):
        add_term(n, dot(t_ref[...], dqkv_ref[:, n * 256 : n * 256 + 256]))
    dqkv_out.wait()
    for store in stores:
        store.wait()


def last_kernel(
    info_ref, n4t_hbm, mine_hbm, theirs_hbm, x_hbm, dblock_hbm, dqkv_hbm, wqkv_hbm,
    keep_ref, s1_ref, s2_ref, s3_ref, out_ref,
    t_ref, dn_ref, n4t_ref, mine_ref, theirs_ref, x_ref, dblock_ref, dqkv_ref, wqkv_ref, in_sems,
):
    loads = copies(
        [
            (n4t_hbm, n4t_ref), (mine_hbm, mine_ref), (theirs_hbm, theirs_ref), (dqkv_hbm, dqkv_ref),
            (wqkv_hbm, wqkv_ref), (x_hbm, x_ref), (dblock_hbm, dblock_ref),
        ],
        in_sems,
    )
    for load in loads:
        load.start()
    for load in loads[:3]:
        load.wait()
    core, y_mine, x_mine = info_ref[1], info_ref[2], info_ref[3]
    source = [lax.rem(x_mine + 4 - k, 4) * 2 + c for c in (core, 1 - core) for k in range(4)]
    for n in range(2):
        cols = slice(n * 512, n * 512 + 512)
        right = jnp.concatenate([r[:, :, cols].reshape(512, 512) for r in (mine_ref, theirs_ref)], axis=0)
        for y in range(4):
            left = jnp.concatenate([n4t_ref[s, y].reshape(64, 128) for s in source], axis=1)
            t_ref[y, :, cols] = dot(left, right)
    keep_ref[...] = t_ref[y_mine]
    for by, ref in ((1, s1_ref), (2, s2_ref), (3, s3_ref)):
        ref[...] = t_ref[lax.rem(y_mine + by, 4)].astype(BF16)

    for load in loads[3:]:
        load.wait()
    for n in range(2):
        cols = slice(n * 256, n * 256 + 256)
        dn_ref[:, cols] = dot_nt(dqkv_ref[...], wqkv_ref[cols, :]).astype(BF16)

    @pl.loop(0, 4)
    def _(w):
        x = x_ref[w].reshape(128, D).astype(F32)
        c = x - jnp.mean(x, axis=-1, keepdims=True)
        r = lax.rsqrt(jnp.mean(c * c, axis=-1, keepdims=True) + EPS)
        y = c * r
        dy = dn_ref[pl.ds(w * 128, 128), :].astype(F32)
        m1 = jnp.mean(dy, axis=-1, keepdims=True)
        m2 = jnp.mean(dy * y, axis=-1, keepdims=True)
        dx = r * (dy - m1 - y * m2)
        out_ref[w] = (dblock_ref[w].reshape(128, D).astype(F32) + dx).astype(BF16).reshape(4, 32, D)


def ring(axes, by):
    count = lax.axis_size(axes)
    return [(i, (i + by) % count) for i in range(count)]


def diagonal(by):
    lats, lons = lax.axis_size(LAT), lax.axis_size("zl")
    return [
        (i * lons + j, (i + by) % lats * lons + (j + by) % lons)
        for i in range(lats)
        for j in range(lons)
    ]


def as_fields(t):
    r, n = t.shape[:2]
    return t.reshape(r, n, 2, 2, D).transpose(0, 1, 3, 2, 4).reshape(r, 2 * n, 2, D)


def as_merged(t):
    r, n = t.shape[:2]
    return t.reshape(r, n // 2, 2, 2, D).transpose(0, 1, 3, 2, 4).reshape(r, n // 2, 2, 2 * D)


def pack(f, m):
    return jnp.concatenate([f, as_fields(m)], axis=0)


def tokens_of(t):
    return t.reshape(2, 2, 4, 4, 2, 2, D).transpose(2, 4, 1, 0, 3, 5, 6).reshape(4, 4, 16, D)


def halo_in(f, m):
    below, f, m = lax.optimization_barrier((pack(f[:4, 4:], m[:2, 2:]), f, m))
    below = lax.ppermute(below, LAT, ring(LAT, -1))
    corner = lax.ppermute(pack(f[:4, :4], m[:2, :2]), ALL, diagonal(-1))
    right = lax.ppermute(pack(f[4:, :4], m[2:, :2]), "zl", ring("zl", -1))
    top = tokens_of(jnp.concatenate([f[4:, 4:], right[:4]], axis=1))
    bottom = tokens_of(jnp.concatenate([below[:4], corner[:4]], axis=1))
    m_top = jnp.concatenate([m[2:, 2:], as_merged(right[4:])], axis=1)
    m_bottom = jnp.concatenate([as_merged(below[4:]), as_merged(corner[4:])], axis=1)
    return top, bottom, jnp.concatenate([m_top, m_bottom], axis=0)


def halo_out(t, h):
    w = t.shape[1] - h
    first, t = lax.optimization_barrier((t[h:, :w], t))
    above = lax.ppermute(first, LAT, ring(LAT, 1))
    corner = lax.ppermute(t[h:, w:], ALL, diagonal(1))
    left = lax.ppermute(t[:h, w:], "zl", ring("zl", 1))
    top = jnp.concatenate([corner, above], axis=1)
    bottom = jnp.concatenate([left, t[:h, :w]], axis=1)
    return jnp.concatenate([top, bottom], axis=0)


def swap_cores(t):
    return lax.ppermute(t, "c", [(0, 1), (1, 0)])


def call(kernel, outs, scratch, flops, *args):
    smem = pl.BlockSpec(memory_space=pltpu.SMEM)
    vmem = pl.BlockSpec(memory_space=pltpu.VMEM)
    hbm = pl.BlockSpec(memory_space=pl.ANY)
    args = [a if isinstance(a, tuple) else (a, False) for a in args]
    return pl.pallas_call(
        kernel,
        out_shape=[jax.ShapeDtypeStruct(shape, dtype) for shape, dtype, _ in outs],
        in_specs=[smem if a.dtype == jnp.int32 else hbm if far else vmem for a, far in args],
        out_specs=[hbm if far else vmem for _, _, far in outs],
        scratch_shapes=[pltpu.SemaphoreType.DMA((t,)) if isinstance(t, int) else pltpu.VMEM(*t) for t in scratch],
        compiler_params=pltpu.CompilerParams(vmem_limit_bytes=LIMIT),
        cost_estimate=pl.CostEstimate(flops=flops, bytes_accessed=1000, transcendentals=0),
    )(*[a for a, _ in args])


def local(fields, qkv_weight, out_weight, merge_weight, cotangent):
    pole = (lax.axis_index(LAT) == lax.axis_size(LAT) - 1).astype(jnp.int32)
    info = jnp.stack([pole] + [lax.axis_index(axis).astype(jnp.int32) for axis in ("c", "y", "x")])
    top, bottom, rolled_cot = halo_in(fields, cotangent)
    cot = rolled_cot.reshape(4, 4, 4, 2, 1024).transpose(1, 0, 2, 3, 4).reshape(128, 1024)
    cells, square = ((4, 4, 32, D), BF16), ((512, 512), BF16)
    wide, probabilities, quarters = ((512, 1536), BF16), ((4, 4, 256, 128), F32), ((8, 4, 2, 32, 128), BF16)
    kept = [cells, square, wide, probabilities, square, cells, quarters]
    x, normed, qkv, probs, att, d_block, n4t, merged = call(
        forward_kernel,
        [(*t, True) for t in kept] + [((128, 1024), BF16, False)],
        [wide, square, ((2048, 1024), BF16), *kept, cells, ((128, 2048), BF16), 3, 7],
        15000000000,
        info, top, bottom, cot, (qkv_weight, True), (out_weight, True), (merge_weight, True),
    )
    cot, d_block = lax.optimization_barrier((cot, d_block))
    cot_mine = jnp.stack([cot] + [lax.ppermute(cot, "x", ring("x", by)) for by in (1, 2, 3)])
    n4t = lax.all_to_all(n4t, XC, 0, 0)
    merged = merged.reshape(4, 4, 4, 2, 1024).transpose(1, 0, 2, 3, 4).reshape(4, 16, 2, 1024)
    part = ((4, 4, 2, 8, 2048), F32, True)
    d_qkv, term_keep, term_send = call(
        backward_kernel,
        [(*wide, True), part, part],
        [square, ((2, 4, 4, 2, 8, 2048), F32), square, square, wide, probabilities, square, cells, square, wide, 6, 1, 16],
        12800000000,
        info, *((t, True) for t in (normed, qkv, probs, att, d_block, out_weight)),
    )
    term_send, n4t, cot_mine = lax.optimization_barrier((term_send, n4t, cot_mine))
    term = (term_keep + swap_cores(term_send)).astype(BF16).reshape(16, 2, 8, 2048)
    term, d_qkv, n4t, merged, cot_mine = lax.optimization_barrier((term, d_qkv, n4t, merged, cot_mine))
    cot_theirs = swap_cores(cot_mine)
    term_got = lax.all_to_all(term, YX, 0, 0)
    group = ((4, 128, 1024), BF16)
    m, s1, s2, s3, field_grad = call(
        last_kernel,
        [((64, 1024), F32, False)] + [((64, 1024), BF16, False)] * 3 + [(*cells, False)],
        [((4, 64, 1024), F32), square, quarters, group, group, cells, cells, wide, wide, 7],
        1000000,
        info, *((t, True) for t in (n4t, cot_mine, cot_theirs, x, d_block, d_qkv, qkv_weight)),
    )
    for by, piece in ((1, s1), (2, s2), (3, s3)):
        m = m + lax.ppermute(piece, "y", ring("y", by)).astype(F32)
    field_grad = field_grad.reshape(4, 2, 2, 4, 4, 2, D).transpose(3, 2, 0, 4, 1, 5, 6).reshape(8, 32, 2, D)
    field_grad = halo_out(field_grad, 4)
    merged = halo_out(merged, 2)
    term_got, m, field_grad = lax.optimization_barrier((term_got, m, field_grad))

    m = m.reshape(2, 32, 4, 256).transpose(0, 2, 1, 3).reshape(8, 32, 256)
    q = jnp.sum(term_got.astype(F32), axis=0)
    qa = q[..., :1536].reshape(2, 8, 4, 384).transpose(0, 2, 1, 3)
    qb = q[..., 1536:].reshape(2, 8, 4, 128).transpose(0, 2, 1, 3)
    q = jnp.concatenate([qa[..., :256], jnp.concatenate([qa[..., 256:], qb], axis=-1)], axis=2).reshape(8, 16, 256)
    both = jnp.concatenate([m, q], axis=1)
    both = jnp.sum(lax.all_to_all(both, Z, 0, 0), axis=0)
    merge_grad = both[:32]
    qkv_grad = jnp.concatenate([both[32:40], both[40:48, :128]], axis=-1)
    out_grad = both[40:48, 128:]
    return (merged, field_grad, qkv_grad, out_grad, merge_grad)


def solution(mesh):
    fine = Mesh(mesh.devices.reshape(4, 2, 4, 2, 4), ALL)
    tokens = P(LAT, "zl", None, None)
    grads = P(LAT, "zl")
    return jax.shard_map(
        local,
        mesh=fine,
        in_specs=(tokens, P(), P(), P(), tokens),
        out_specs=(tokens, tokens, grads, grads, grads),
        check_vma=False,
    )
```
